32 devices in a mesh: gx: 8 (over y, x, core), gy: 4 (over z).
Axes of the slice: x: 2, y: 2, z: 4, core: 2. Of those that a mesh axis runs over, the one named last changes fastest.
Arguments:
- atmosphere_state: bfloat16 [128, 800, 1600], P('gy', 'gx'), may hold values from -6 to 6
- forcing: float32 [128], P('gy'), may hold values from -4 to 4
- mixing: float32 [4, 32, 32], replicated, may hold values from -1 to 1
- order_slot: int32 [800], replicated, may hold values from 0 to 799, each once
- legendre: bfloat16 [800, 800, 800], P('gx', None, 'gy'), may hold values from -0.21875 to 0.21875
- ocean_tracer: float32 [8, 256, 2048], P(None, 'gy', 'gx'), may hold values from -6 to 6
- kinetic: float32 [8, 256, 2048], P(None, 'gy', 'gx'), may hold values from 0.01 to 1
- dissipation: float32 [8, 256, 2048], P(None, 'gy', 'gx'), may hold values from 0.001 to 0.1
- wet_mask: int32 [256, 2048], P('gy', 'gx'), may hold values 0 or 1
- send_cell: int32 [4, 10240], P('gy', 'gx'), may hold values from 0 to 16383
- send_weight: float32 [4, 10240], P('gy', 'gx'), may hold values from 0.5 to 2
- receive_cell: int32 [4, 10240], P('gy', 'gx'), may hold values from 0 to 159999
- wind_source: int32 [4, 10240], P('gy', 'gx'), may hold values from 0 to 159999
- wind_target: int32 [4, 10240], P('gy', 'gx'), may hold values from 0 to 16383
- wind_count: int32 [4, 8, 8], P('gy', 'gx'), may hold values from 1 to 160, 640 in all within a row
Outputs:
- spectral: float32 [800, 800, 256], P('gx', 'gy')
- tracer_out: float32 [8, 256, 2048], P(None, 'gy', 'gx')
The draws below stay inside these ranges and needn't reach their ends.
Inputs may be any that keep to these rules, and one draw needn't show every extreme that they name: `wind_count`: for every tile some band sends exactly 160 live slots.
All inputs are finite; a program needn't handle non-finite values. No bound on the sum of `wet_mask` on one device may be relied on, other than what follows from the above.
Results may differ from the reference program's by a relative error of at most 0.0035.
The reference program's roundings to bfloat16 on the way (of `forced`, `wind`, `table` and `fourier`) count: a program that leaves them out, or rounds other values in their place, can miss the bound.
Values may be sent and summed in bfloat16 or wider, within the bound.
A program may use at most 192 MiB of HBM per device.

```python
import math
import jax
import jax.numpy as jnp
import numpy as np
from jax import lax

NLAT = 800
NLON = 1600
ORDERS = 800
NDEG = 800
NVAR = 4
LEV = 32
OLAY = 8
OSTEPS = 4
OCEAN_TILE_ROWS = 64
OCOL_DEV = 256
CAP = 160
RCAP = 160
FIELDS = 128
LAT_DEV = 100
ORD_DEV = 100
OROWS = 256
OCOLS = 2048
N_GX = 8
N_GY = 4


def touch_ends(drawn, own_key, smallest, largest):
    spot = [jax.random.randint(jax.random.fold_in(own_key, axis), (), 0, length) for axis, length in enumerate(drawn.shape)]
    widest = drawn.shape.index(max(drawn.shape))
    neighbour = spot[:widest] + [(spot[widest] + 1) % drawn.shape[widest]] + spot[widest + 1:]
    return drawn.at[tuple(spot)].set(smallest).at[tuple(neighbour)].set(largest)


def shard_levels(stream_key, shape, pieces, smallest, largest):
    gain = 1.0
    for axis_at, shards_of in pieces:
        draws = jax.random.uniform(jax.random.fold_in(jax.random.fold_in(stream_key, 6), axis_at), (shards_of,), jnp.float32, smallest / len(pieces), largest / len(pieces))
        gain = gain * jnp.repeat(jnp.exp(draws), shape[axis_at] // shards_of).reshape((-1,) + (1,) * (len(shape) - 1 - axis_at))
    return gain


def length_profile(amount, total, reach, slope):
    weights = [(1 << 20) // math.isqrt(standing ** slope) + 1 for standing in range(2, amount + 1)]
    rest, given = total - reach - (amount - 1), [1] * (amount - 1)
    while rest > 0:
        free = [i for i in range(amount - 1) if given[i] < reach]
        mass, left = sum([weights[i] for i in free]), rest
        for i in free:
            extra = min(reach - given[i], max(1, left * weights[i] // mass), rest)
            given[i] = given[i] + extra
            rest = rest - extra
    return np.array([reach] + given)


def ragged(stream_key, number_of, total, limit, slope):
    if number_of == 2:
        one = jax.random.randint(stream_key, (), max(1, total - limit), min(limit, total - 1) + 1)
        return jnp.stack([one, total - one])
    lengths = jnp.asarray(length_profile(number_of, total, limit, slope), jnp.int32)
    couples = (number_of - 1) // 2
    source_of, receiver = lengths[1:1 + 2 * couples:2], lengths[2:2 + 2 * couples:2]
    slack = jnp.minimum(source_of - 1, limit - receiver)
    passed = jax.random.randint(jax.random.fold_in(stream_key, 1), (couples,), 0, 1 << 20) % (slack + 1)
    lengths = lengths.at[1:1 + 2 * couples:2].set(source_of - passed).at[2:2 + 2 * couples:2].set(receiver + passed)
    return lengths[jax.random.permutation(jax.random.fold_in(stream_key, 2), number_of)]


def bell_draw(stream_key, extent, width, bound, shards=(), kind=jnp.bfloat16):
    entries = width * jax.random.normal(stream_key, extent, jnp.float32)
    if shards:
        entries = entries * shard_levels(stream_key, extent, shards, -0.22, 0.18)
    return jnp.clip(entries, -bound, bound).astype(kind)


def setup_inputs(seed: int = 0) -> dict:
    keys = jax.random.split(jax.random.key(seed), 16)
    return {
        "atmosphere_state": bell_draw(keys[0], (FIELDS, NLAT, NLON), 1.0, 6.0, ((0, 4), (1, 8))),
        "forcing": bell_draw(keys[1], (FIELDS,), 1.0, 4.0, ((0, 4),), jnp.float32),
        "mixing": bell_draw(keys[2], (NVAR, LEV, LEV), LEV ** -0.5, 1.0, (), jnp.float32),
        "order_slot": jax.random.permutation(keys[3], ORDERS).astype(jnp.int32),
        "legendre": bell_draw(keys[4], (ORDERS, NLAT, NDEG), NLAT ** -0.5, 0.21875, ((0, 8), (2, 4))),
        "ocean_tracer": bell_draw(keys[5], (OLAY, OROWS, OCOLS), 1.0, 6.0, ((1, 4), (2, 8)), jnp.float32),
        "kinetic": jnp.clip(jnp.exp(math.log(1.0) - 4.6051702 * jax.random.uniform(keys[6], (OLAY, OROWS, OCOLS), jnp.float32) ** shard_levels(keys[6], (OLAY, OROWS, OCOLS), ((1, 4), (2, 8)), -0.2, 0.2)), 0.01, 1.0),
        "dissipation": jnp.clip(jnp.exp(math.log(0.1) - 4.6051702 * jax.random.uniform(keys[7], (OLAY, OROWS, OCOLS), jnp.float32) ** shard_levels(keys[7], (OLAY, OROWS, OCOLS), ((1, 4), (2, 8)), -0.2, 0.2)), 0.001, 0.1),
        "wet_mask": touch_ends((jax.random.randint(keys[8], (OROWS, OCOLS), 0, 10) < 7).astype(jnp.int32), jax.random.fold_in(keys[8], 1), 0, 1),
        "send_cell": touch_ends(jax.random.randint(keys[9], (N_GY, N_GX * N_GX * CAP), 0, OCEAN_TILE_ROWS * OCOL_DEV), jax.random.fold_in(keys[9], 1), 0, (OCEAN_TILE_ROWS * OCOL_DEV) - 1).astype(jnp.int32),
        "send_weight": jnp.clip(jnp.exp(math.log(2.0) - 1.3862944 * jax.random.uniform(keys[10], (N_GY, N_GX * N_GX * CAP), jnp.float32) ** shard_levels(keys[10], (N_GY, N_GX * N_GX * CAP), ((0, 4), (1, 8)), -0.2, 0.2)), 0.5, 2.0),
        "receive_cell": touch_ends(jax.random.randint(keys[11], (N_GY, N_GX * N_GX * CAP), 0, LAT_DEV * NLON), jax.random.fold_in(keys[11], 1), 0, (LAT_DEV * NLON) - 1).astype(jnp.int32),
        "wind_source": touch_ends(jax.random.randint(keys[12], (N_GY, N_GX * N_GX * RCAP), 0, LAT_DEV * NLON), jax.random.fold_in(keys[12], 1), 0, (LAT_DEV * NLON) - 1).astype(jnp.int32),
        "wind_target": touch_ends(jax.random.randint(keys[13], (N_GY, N_GX * N_GX * RCAP), 0, OCEAN_TILE_ROWS * OCOL_DEV), jax.random.fold_in(keys[13], 1), 0, (OCEAN_TILE_ROWS * OCOL_DEV) - 1).astype(jnp.int32),
        "wind_count": jax.vmap(lambda own: ragged(own, N_GX, N_GX * RCAP // 2, RCAP, 2))(jax.random.split(keys[14], N_GY * N_GX)).reshape((N_GY, N_GX, N_GX)).astype(jnp.int32),
    }


mix_coeff = 0.12
wind_coeff = 0.5

def order_table(order_slot, longitudes):
    lon_index = jnp.arange(longitudes, dtype=jnp.int32)
    phase = lon_index[:, None] * order_slot[None, :].astype(jnp.int32) % longitudes
    angle = phase.astype(jnp.float32) * (2.0 * math.pi / longitudes)
    scale = 1.0 / math.sqrt(longitudes)
    return jnp.stack([jnp.cos(angle) * scale, -jnp.sin(angle) * scale], axis=1).astype(jnp.bfloat16)

def relax(tracer, wetf, vface, padded):
    layers = tracer.shape[0]
    rows = tracer.shape[1]
    cols = tracer.shape[2]
    change = jnp.zeros_like(tracer)
    for row_shift, col_shift in ((0, 1), (2, 1), (1, 0), (1, 2)):
        nearby = padded[:, row_shift:row_shift + rows, col_shift:col_shift + cols]
        change = change + mix_coeff * wetf * nearby[layers] * (nearby[:layers] - tracer)
    flux = vface * (tracer[1:] - tracer[:-1])
    change = change.at[:-1].add(flux).at[1:].add(-flux)
    return tracer + change

def reference(atmosphere_state, forcing, mixing, order_slot, legendre, ocean_tracer, kinetic, dissipation, wet_mask, send_cell, send_weight, receive_cell, wind_source, wind_target, wind_count):
    band_cells = LAT_DEV * NLON
    tile_cells = OCEAN_TILE_ROWS * OCOL_DEV
    wetf = wet_mask.astype(jnp.float32)

    def scatter_to_tiles(field):
        return field.reshape(N_GY, OCEAN_TILE_ROWS, N_GX, OCOL_DEV).transpose(0, 2, 1, 3).reshape(N_GY, N_GX, tile_cells)

    def from_tiles(field):
        return field.reshape(N_GY, N_GX, OCEAN_TILE_ROWS, OCOL_DEV).transpose(0, 2, 1, 3).reshape(OROWS, OCOLS)
    sea = scatter_to_tiles(ocean_tracer[0] * wetf)
    row_pick = jnp.arange(N_GY, dtype=jnp.int32)[:, None, None, None]
    col_pick = jnp.arange(N_GX, dtype=jnp.int32)[None, :, None, None]
    offers = sea[row_pick, col_pick, send_cell.reshape(N_GY, N_GX, N_GX, CAP)] * send_weight.reshape(N_GY, N_GX, N_GX, CAP)
    arrived = offers.transpose(0, 2, 1, 3)
    band_pick = jnp.arange(N_GX, dtype=jnp.int32)[None, :, None, None]
    target_cells = band_pick * band_cells + receive_cell.reshape(N_GY, N_GX, N_GX, CAP)
    surface_fields = jnp.zeros((NLAT * NLON,), jnp.float32).at[target_cells.reshape(-1)].add(arrived.reshape(-1)).reshape(NLAT, NLON)
    forced = (atmosphere_state.astype(jnp.float32) + forcing[:, None, None] * surface_fields[None]).astype(jnp.bfloat16)
    lower = forced[:2 * LEV].astype(jnp.float32).reshape(2, LEV, NLAT * NLON)
    wind = jnp.einsum('wl,wlc->wc', mixing[:2, 0, :], lower, precision=lax.Precision.HIGHEST).astype(jnp.bfloat16)
    table = order_table(order_slot, NLON).reshape(NLON, 2 * ORDERS)
    fourier = jnp.einsum('fal,lc->fca', forced.astype(jnp.float32), table.astype(jnp.float32)).astype(jnp.bfloat16)
    four_blocks = fourier.reshape(FIELDS, 2, N_GX, ORD_DEV, NLAT).transpose(2, 0, 1, 3, 4)
    legendre_blocks = legendre.reshape(N_GX, ORD_DEV, NLAT, NDEG)
    order_blocks = order_slot.reshape(N_GX, ORD_DEV)
    degree = jnp.arange(NDEG, dtype=jnp.int32)

    def one_block(inputs):
        four_part, table_part, order_part = inputs
        masked = jnp.where(degree[None, None, :] >= order_part[:, None, None], table_part, jnp.zeros_like(table_part))
        unmixed_values = jnp.einsum('frsl,sln->snfr', four_part.astype(jnp.float32), masked.astype(jnp.float32))
        unmixed_values = unmixed_values.reshape(ORD_DEV, NDEG, NVAR, LEV, 2)
        mixed_tracer = jnp.einsum('hkz,fchzu->fchku', mixing, unmixed_values, precision=lax.Precision.HIGHEST)
        return mixed_tracer.reshape(ORD_DEV, NDEG, FIELDS * 2)
    spectral = lax.map(one_block, (four_blocks, legendre_blocks, order_blocks)).reshape(ORDERS, NDEG, FIELDS * 2)
    source_band = jnp.arange(N_GX, dtype=jnp.int32)[None, None, :, None]
    global_cell = source_band * band_cells + wind_source.reshape(N_GY, N_GX, N_GX, RCAP)
    fetched = wind[:, global_cell].astype(jnp.float32)
    live = (jnp.arange(RCAP, dtype=jnp.int32)[None, None, None, :] < wind_count[:, :, :, None]).astype(jnp.float32)
    tile_pick = (jnp.arange(N_GY, dtype=jnp.int32)[:, None, None, None] * N_GX + jnp.arange(N_GX, dtype=jnp.int32)[None, :, None, None]) * tile_cells
    placed = tile_pick + wind_target.reshape(N_GY, N_GX, N_GX, RCAP)
    ocean_wind = jnp.zeros((2, N_GY * N_GX * tile_cells), jnp.float32).at[:, placed.reshape(-1)].add((fetched * live[None]).reshape(2, -1))
    east_wind = from_tiles(ocean_wind[0])
    north_wind = from_tiles(ocean_wind[1])
    speed = east_wind ** 2 + north_wind ** 2
    energy = kinetic.at[0].add(wind_coeff * speed)
    ratio = 0.09 * energy * energy / dissipation
    viscosity = 0.25 * ratio / (1.0 + ratio)
    vface = 0.5 * (viscosity[:-1] + viscosity[1:]) * wetf[None]
    tracer = ocean_tracer
    for sub_step in range(OSTEPS):
        stacked = jnp.concatenate([tracer, wetf[None]], axis=0)
        padded = jnp.pad(stacked, ((0, 0), (1, 1), (1, 1)))
        tracer = relax(tracer, wetf, vface, padded)
    return (spectral, tracer)
```

```python
import functools
import math

import jax
import jax.numpy as jnp
from jax import lax
from jax.experimental import pallas as pl
from jax.experimental.pallas import tpu as pltpu
from jax.sharding import PartitionSpec as P

OSTEPS = 4


mix_coeff = 0.12
wind_coeff = 0.5


def with_halo(x, sides, width):
    for axis, dim in sides:
        peers, length = (lax.axis_size(axis), x.shape[dim])
        up = [(i, (i + 1) % peers) for i in range(peers - 1)]
        down = [(j, i) for i, j in up]
        last = lax.slice_in_dim(x, length - width, length, axis=dim)
        first = lax.slice_in_dim(x, 0, width, axis=dim)
        before = lax.ppermute(last, axis, up)
        after = lax.ppermute(first, axis, down)
        x = jnp.concatenate([before, x, after], axis=dim)
    return x


def order_table(order_slot, longitudes):
    product = jnp.arange(longitudes, dtype=jnp.float32)[:, None] * order_slot.astype(jnp.float32)[None, :]
    k = product - longitudes * jnp.round(product * (1.0 / longitudes))
    x = (jnp.abs(k) * (2.0 / longitudes) - 0.5) * math.pi
    y = x * x
    scale = 1.0 / math.sqrt(longitudes)
    sine = sum_series(y, [(-1) ** i * scale / math.factorial(2 * i + 1) for i in range(7)]) * x
    cosine = sum_series(y, [(-1) ** i * scale / math.factorial(2 * i) for i in range(8)])
    return (-sine).astype(jnp.bfloat16), jnp.where(k < 0, cosine, -cosine).astype(jnp.bfloat16)


def sum_series(y, terms):
    total = jnp.full_like(y, terms[-1])
    for term in terms[-2::-1]:
        total = total * y + term
    return total


def relax(tracer, wetf, vface, padded):
    layers = tracer.shape[0]
    rows = tracer.shape[1]
    cols = tracer.shape[2]
    change = jnp.zeros_like(tracer)
    for row_shift, col_shift in ((0, 1), (2, 1), (1, 0), (1, 2)):
        nearby = padded[:, row_shift : row_shift + rows, col_shift : col_shift + cols]
        change = change + mix_coeff * wetf * nearby[layers] * (nearby[:layers] - tracer)
    flux = vface * (tracer[1:] - tracer[:-1])
    change = change.at[:-1].add(flux).at[1:].add(-flux)
    return tracer + change


PAIRS = 4
LAG = 2
AHEAD = 3
MESH = pl.DeviceIdType.MESH


def spectral_kernel(
    nx, nz, chunks, four_ref, leg_ref, mix_ref, order_ref, out_ref,
    held, legs, outs, own_sem, a_send, a_recv, z_send, z_recv, leg_sem, out_sem,
):
    me_x = lax.axis_index("gx")
    me_z = lax.axis_index("gy")
    own_orders, lats, degrees = leg_ref.shape
    band = lats // nx
    per_chunk = 2 * PAIRS

    barrier = pltpu.get_barrier_semaphore()
    for d in range(1, nx):
        pl.semaphore_signal(
            barrier, inc=1, device_id=(lax.rem(me_x + d, nx), me_z), device_id_type=MESH
        )

    @pl.when(me_z > 0)
    def _():
        pl.semaphore_signal(barrier, inc=1, device_id=(me_x, me_z - 1), device_id_type=MESH)

    @pl.when(me_z < nz - 1)
    def _():
        pl.semaphore_signal(barrier, inc=1, device_id=(me_x, me_z + 1), device_id_type=MESH)

    beside = jnp.where(me_z > 0, 1, 0) + jnp.where(me_z < nz - 1, 1, 0)
    pl.semaphore_wait(barrier, nx - 1 + beside)

    def own_copy(c):
        return pltpu.make_async_copy(
            four_ref.at[me_x, c], held.at[c, me_z, me_x], own_sem.at[c]
        )

    def band_copy(c, d):
        peer = lax.rem(me_x + d, nx)
        return pltpu.make_async_remote_copy(
            src_ref=four_ref.at[peer, c],
            dst_ref=held.at[c, me_z, me_x],
            send_sem=a_send.at[c, d],
            recv_sem=a_recv.at[c, d],
            device_id=(peer, me_z),
            device_id_type=MESH,
        )

    def group_copy(way, hop, c):
        step = 1 if way == 0 else -1
        group = me_z - step * hop
        return pltpu.make_async_remote_copy(
            src_ref=held.at[c, group],
            dst_ref=held.at[c, group],
            send_sem=z_send.at[way, hop, c],
            recv_sem=z_recv.at[way, hop, c],
            device_id=(me_x, me_z + step),
            device_id_type=MESH,
        )

    def arrived(way, hop, c):
        step = 1 if way == 0 else -1
        group = me_z - step * (hop + 1)
        pltpu.make_async_copy(
            held.at[c, group], held.at[c, group], z_recv.at[way, hop, c]
        ).wait()

    def leg_copy(s, slot):
        return pltpu.make_async_copy(leg_ref.at[s], legs.at[slot], leg_sem.at[slot])

    def out_copy(s, slot):
        return pltpu.make_async_copy(outs.at[slot], out_ref.at[s], out_sem.at[slot])

    def send_bands(c):
        own_copy(c).start()
        for d in range(1, nx):
            band_copy(c, d).start()

    leg_copy(0, 0).start()
    for c in range(min(AHEAD, chunks)):
        send_bands(c)

    def contract(c):
        for q in range(PAIRS):
            rows = slice(q * band, (q + 1) * band)

            def one_order(s2, carry):
                s = c * per_chunk + 2 * q + s2

                @pl.when(s < own_orders)
                def _():
                    leg_copy(s, s2).wait()

                    @pl.when(s + 1 < own_orders)
                    def _():
                        leg_copy(s + 1, 1 - s2).start()

                    raw = jnp.zeros((degrees, nz * 128), jnp.float32)
                    for b in range(nx):
                        block = jnp.concatenate(
                            [held[c, g, b, rows, :] for g in range(nz)], axis=1
                        )
                        raw = raw + lax.dot_general(
                            legs[s2, b * band : (b + 1) * band, :],
                            block,
                            (((0,), (0,)), ((), ())),
                            preferred_element_type=jnp.float32,
                        )
                    degree = me_z * degrees + lax.broadcasted_iota(jnp.int32, raw.shape, 0)
                    raw = jnp.where(degree >= order_ref[me_x * own_orders + s], raw, 0.0)

                    @pl.when(s >= 2)
                    def _():
                        out_copy(s - 2, s2).wait()

                    outs[s2] = jnp.dot(
                        raw,
                        mix_ref[s2],
                        precision=lax.Precision.HIGHEST,
                        preferred_element_type=jnp.float32,
                    )
                    out_copy(s, s2).start()

                return carry

            lax.fori_loop(0, 2, one_order, 0)

    def step(t, carry):
        @pl.when(t + AHEAD < chunks)
        def _():
            send_bands(t + AHEAD)

        @pl.when(t < chunks)
        def _():
            own_copy(t).wait()
            for d in range(1, nx):
                band_copy(t, d).wait_recv()

            @pl.when(me_z < nz - 1)
            def _():
                group_copy(0, 0, t).start()

            @pl.when(me_z > 0)
            def _():
                group_copy(1, 0, t).start()

        for hop in range(1, nz):
            c = t - LAG * hop

            @pl.when((c >= 0) & (c < chunks))
            def _():
                @pl.when(me_z >= hop)
                def _():
                    arrived(0, hop - 1, c)
                    if hop < nz - 1:

                        @pl.when(me_z < nz - 1)
                        def _():
                            group_copy(0, hop, c).start()

                @pl.when(me_z < nz - hop)
                def _():
                    arrived(1, hop - 1, c)
                    if hop < nz - 1:

                        @pl.when(me_z > 0)
                        def _():
                            group_copy(1, hop, c).start()

        last = t - LAG * (nz - 1)

        @pl.when(last >= 0)
        def _():
            contract(last)

        return carry

    lax.fori_loop(0, chunks + LAG * (nz - 1), step, 0)

    out_copy(own_orders - 2, (own_orders - 2) % 2).wait()
    out_copy(own_orders - 1, (own_orders - 1) % 2).wait()

    def finish(c, carry):
        for d in range(1, nx):
            band_copy(c, d).wait_send()
        for hop in range(nz - 1):

            @pl.when((me_z >= hop) & (me_z < nz - 1))
            def _():
                group_copy(0, hop, c).wait_send()

            @pl.when((me_z < nz - hop) & (me_z > 0))
            def _():
                group_copy(1, hop, c).wait_send()

        return carry

    lax.fori_loop(0, chunks, finish, 0)


def spectral_part(forced, mixing, order_slot, legendre):
    nx, nz = lax.axis_size("gx"), lax.axis_size("gy")
    field_rows, band, longitudes = forced.shape
    own_orders, lats, degrees = legendre.shape
    variables, levels = mixing.shape[:2]
    fields = variables * levels
    if field_rows * 4 != 128 or (PAIRS * band) % 16 or own_orders % 2:
        return spectral_plain(forced, mixing, order_slot, legendre)
    chunks = -(-own_orders // (2 * PAIRS))
    padded = chunks * 2 * PAIRS
    slots = jnp.pad(order_slot.reshape(nx, own_orders), ((0, 0), (0, padded - own_orders)))
    pairs = nx * padded // 2
    cosine, sine = order_table(slots.reshape(pairs, 2).T.reshape(-1), longitudes)
    table = jnp.stack([cosine.reshape(longitudes, 2, pairs), sine.reshape(longitudes, 2, pairs)], 2)
    four = jnp.einsum(
        "fal,lqp->paqf", forced, table.reshape(longitudes, 4, pairs), preferred_element_type=jnp.float32
    ).astype(jnp.bfloat16)
    four = four.reshape(nx, chunks, PAIRS * band, 128)
    mix = mixing[:, None, :, :, None] * jnp.eye(variables, dtype=mixing.dtype)[:, :, None, None, None]
    mix = mix.transpose(1, 3, 0, 2, 4).reshape(nz, 1, field_rows, fields, 1)
    mix = mix[:, :, None] * jnp.eye(2, dtype=mixing.dtype)[None, None, :, None, None, :]
    mix = jnp.eye(2, dtype=mixing.dtype)[:, None, :, None, None, None, None] * mix[None]
    mix = mix.reshape(2, nz * 128, fields * 2)
    scratch = [
        pltpu.VMEM((chunks, nz, nx, PAIRS * band, 128), jnp.bfloat16),
        pltpu.VMEM((2, lats, degrees), legendre.dtype),
        pltpu.VMEM((2, degrees, 2 * fields), jnp.float32),
        pltpu.SemaphoreType.DMA((chunks,)),
        pltpu.SemaphoreType.DMA((chunks, nx)),
        pltpu.SemaphoreType.DMA((chunks, nx)),
        pltpu.SemaphoreType.DMA((2, nz - 1, chunks)),
        pltpu.SemaphoreType.DMA((2, nz - 1, chunks)),
        pltpu.SemaphoreType.DMA((2,)),
        pltpu.SemaphoreType.DMA((2,)),
    ]
    return pl.pallas_call(
        functools.partial(spectral_kernel, nx, nz, chunks),
        out_shape=jax.ShapeDtypeStruct((own_orders, degrees, 2 * fields), jnp.float32),
        in_specs=[
            pl.BlockSpec(memory_space=pl.ANY),
            pl.BlockSpec(memory_space=pl.ANY),
            pl.BlockSpec(memory_space=pltpu.VMEM),
            pl.BlockSpec(memory_space=pltpu.SMEM),
        ],
        out_specs=pl.BlockSpec(memory_space=pl.ANY),
        scratch_shapes=scratch,
        compiler_params=pltpu.CompilerParams(
            collective_id=0, has_side_effects=True, vmem_limit_bytes=58 << 20
        ),
    )(four, legendre, mix, order_slot)


def spectral_plain(forced, mixing, order_slot, legendre):
    field_rows, band_rows, longitudes = forced.shape
    variables, levels = mixing.shape[:2]
    orders = order_slot.shape[0]
    table = jnp.stack(order_table(order_slot, longitudes), axis=1).reshape(longitudes, 2 * orders)
    fourier = jnp.einsum("fal,lc->fca", forced, table, preferred_element_type=jnp.float32).astype(
        jnp.bfloat16
    )
    fourier = fourier.reshape(field_rows, 2, orders, band_rows)
    own_orders = legendre.shape[0]
    own_degrees = legendre.shape[2]
    my_orders = lax.dynamic_slice_in_dim(
        order_slot, lax.axis_index("gx") * own_orders, own_orders, 0
    )
    degree = lax.axis_index("gy") * own_degrees + jnp.arange(own_degrees, dtype=jnp.int32)
    masked = jnp.where(
        degree[None, None, :] >= my_orders[:, None, None], legendre, jnp.zeros_like(legendre)
    )
    moved = lax.all_to_all(fourier, "gx", split_axis=2, concat_axis=3, tiled=True)
    unmixed_values = jnp.einsum(
        "frsl,sln->snfr",
        lax.all_gather(moved, "gy", axis=0, tiled=True),
        masked,
        preferred_element_type=jnp.float32,
    )
    unmixed_values = unmixed_values.reshape(own_orders, own_degrees, variables, levels, 2)
    mixed_tracer = jnp.einsum(
        "hkz,fchzu->fchku", mixing, unmixed_values, precision=lax.Precision.HIGHEST
    )
    return mixed_tracer.reshape(own_orders, own_degrees, variables * levels * 2)


def shards(
    atmosphere_state,
    forcing,
    mixing,
    order_slot,
    legendre,
    ocean_tracer,
    kinetic,
    dissipation,
    wet_mask,
    send_cell,
    send_weight,
    receive_cell,
    wind_source,
    wind_target,
    wind_count,
):
    bands = lax.axis_size("gx")
    field_rows, band_rows, longitudes = atmosphere_state.shape
    band_cells = band_rows * longitudes
    layers, tile_rows, tile_cols = ocean_tracer.shape
    tile_cells = tile_rows * tile_cols
    variables = mixing.shape[0]
    levels = mixing.shape[1]
    wetf = wet_mask.astype(jnp.float32)
    sea_top = (ocean_tracer[0] * wetf).reshape(tile_cells)
    offers = sea_top[send_cell.reshape(bands, -1)] * send_weight.reshape(bands, -1)
    arrived = lax.all_to_all(offers, "gx", split_axis=0, concat_axis=0, tiled=True)
    partial_surface = (
        jnp.zeros((band_cells,), jnp.float32).at[receive_cell.reshape(-1)].add(arrived.reshape(-1))
    )
    surface_fields = lax.psum(partial_surface, "gy").reshape(band_rows, longitudes)
    forced = (
        atmosphere_state.astype(jnp.float32) + forcing[:, None, None] * surface_fields[None]
    ).astype(jnp.bfloat16)
    offset = lax.axis_index("gy") * field_rows
    select = (jnp.arange(variables)[None, :] == jnp.arange(2)[:, None]).astype(jnp.float32)
    bottom = (select[:, :, None] * mixing[None, :, 0, :]).reshape(2, variables * levels)
    bottom_rows = lax.dynamic_slice_in_dim(bottom, offset, field_rows, 1)
    partial_wind_stress = jnp.dot(
        bottom_rows,
        forced.reshape(field_rows, band_cells).astype(jnp.float32),
        precision=lax.Precision.HIGHEST,
    )
    wind = lax.psum(partial_wind_stress.astype(jnp.bfloat16), "gy")
    spectral = spectral_part(forced, mixing, order_slot, legendre)
    sources = wind_source.reshape(bands, -1)
    slots = sources.shape[1]
    every_band = lax.all_gather(wind, "gx", axis=1, tiled=True)
    global_cell = jnp.arange(bands, dtype=jnp.int32)[:, None] * band_cells + sources
    fetched = every_band[:, global_cell]
    live = (
        jnp.arange(slots, dtype=jnp.int32)[None, :] < wind_count.reshape(bands)[:, None]
    ).astype(jnp.float32)
    ocean_wind = (
        jnp.zeros((2, tile_cells), jnp.float32)
        .at[:, wind_target.reshape(-1)]
        .add((fetched.astype(jnp.float32) * live[None]).reshape(2, -1))
    )
    east_wind = ocean_wind[0].reshape(tile_rows, tile_cols)
    north_wind = ocean_wind[1].reshape(tile_rows, tile_cols)
    speed = east_wind**2 + north_wind**2
    energy = kinetic.at[0].add(wind_coeff * speed)
    ratio = 0.09 * energy * energy / dissipation
    viscosity = 0.25 * ratio / (1.0 + ratio)
    vface = 0.5 * (viscosity[:-1] + viscosity[1:]) * wetf[None]
    tracer = ocean_tracer
    for sub_step in range(OSTEPS):
        stacked = jnp.concatenate([tracer, wetf[None]], axis=0)
        padded = with_halo(stacked.astype(jnp.bfloat16), (("gx", 2), ("gy", 1)), 1).astype(
            stacked.dtype
        )
        tracer = relax(tracer, wetf, vface, padded)
    return (spectral, tracer)


def solution(mesh):
    placed = (
        P("gy", "gx", None),
        P("gy"),
        P(),
        P(),
        P("gx", None, "gy"),
        P(None, "gy", "gx"),
        P(None, "gy", "gx"),
        P(None, "gy", "gx"),
        P("gy", "gx"),
        P("gy", "gx"),
        P("gy", "gx"),
        P("gy", "gx"),
        P("gy", "gx"),
        P("gy", "gx"),
        P("gy", "gx", None),
    )
    return jax.shard_map(
        shards,
        mesh=mesh,
        in_specs=placed,
        out_specs=(P("gx", "gy", None), P(None, "gy", "gx")),
        check_vma=False,
    )
```
